512 devices in a mesh: dp: 32 (over y_lo, x, core), seq: 16 (over y_hi, z).
Axes of the slice: x: 4, y: 8 (y_hi: 2, y_lo: 4; y = y_hi * 4 + y_lo), z: 8, core: 2. Of those that a mesh axis runs over, the one named last changes fastest.
Arguments:
- bins: bfloat16 [32, 2048, 1536], P('dp', 'seq'), may hold values from -6 to 6
- pair_in: bfloat16 [32, 128, 128, 128], P('dp', 'seq'), may hold values from -12 to 12
- valid: int32 [32], P('dp'), may hold values from 1024 to 2048, as said below
- gain: float32 [1536], replicated, may hold values from 0.5 to 1.5
- w_qkv: bfloat16 [1536, 2304], P('dp'), may hold values from -0.15625 to 0.15625
- w_pair: bfloat16 [1536, 256], P('dp'), may hold values from -0.15625 to 0.15625
- w_bias: float32 [128, 6], replicated, may hold values from -2 to 2
- w_out: bfloat16 [768, 1536], P(None, 'dp'), may hold values from -0.21875 to 0.21875
Outputs:
- mixed: bfloat16 [32, 2048, 1536], P('dp', 'seq')
- pair_out: bfloat16 [32, 128, 128, 128], P('dp', 'seq')
The draws below stay inside these ranges and needn't reach their ends.
Inputs may be any that keep to these rules, and one draw needn't show every extreme that they name: `valid`: the first window is full.
All inputs are finite; a program needn't handle non-finite values.
Results may differ from the reference program's by a relative error of at most 0.006.
Values may be sent and summed in bfloat16 or wider, within the bound.
No kernel may reach another device: no remote copies, remote signals or barrier semaphores. Data moves between devices by JAX's collectives and lax.ppermute only.
A program may use at most 64 MiB of HBM per device.

```python
import jax
import jax.numpy as jnp
from jax import lax

D = 1536
HEADS = 6
HD = 128
CP = 128
POOL = 16
BINS = 2048
PAIRS = 128
BATCH = 32


def draw_valid(key, part):
    key = jax.random.fold_in(key, 7)
    drawn = jax.random.randint(key, (BATCH,), BINS // 2, BINS + 1)
    return drawn.at[0].set(BINS).astype(jnp.int32)


def draw_pair_in(key, part):
    key = jax.random.fold_in(key, 11)
    base_key = jax.random.fold_in(key, 0)
    base = jnp.clip(jax.random.normal(base_key, (BATCH, PAIRS, PAIRS, CP), jnp.float32), -12.0, 12.0)
    return base.astype(jnp.bfloat16)


def draw_w_bias(key, part):
    key = jax.random.fold_in(key, 13)
    drawn = jnp.clip(jax.random.normal(key, (CP, HEADS), jnp.float32) * CP ** (-0.5), -2.0, 2.0)
    return drawn.astype(jnp.float32)


def level_of(key, dims, pieces, least, top_value):
    def one(axis_at, blocks):
        steps = jax.random.uniform(jax.random.fold_in(jax.random.fold_in(key, 6), axis_at), (blocks,), jnp.float32, least / len(pieces), top_value / len(pieces))
        return jnp.repeat(jnp.exp(steps), dims[axis_at] // blocks).reshape((-1,) + (1,) * (len(dims) - axis_at - 1))

    level = one(*pieces[0])
    for cut in pieces[1:]:
        level = level * one(*cut)
    return level


def noise(stream_key, dims, spread, reach, pieces=(), held_as=jnp.bfloat16):
    values = jax.random.normal(stream_key, dims, jnp.float32) * spread
    if len(pieces) > 0:
        values = level_of(stream_key, dims, pieces, -0.22, 0.18) * values
    return jnp.clip(values, min=-reach, max=reach).astype(held_as)


def setup_inputs(seed: int = 0) -> dict:
    splits = jax.random.split(jax.random.key(seed), 9)
    bins = noise(splits[0], (BATCH, BINS, D), 1.0, 6.0, ((0, 32), (1, 16)))
    pair_in = draw_pair_in(jax.random.fold_in(splits[8], 71), 0)
    valid = draw_valid(jax.random.fold_in(splits[8], 71), 0)
    gain = jnp.clip(1.0 + 0.1 * jax.random.normal(splits[3], (D,), jnp.float32), 0.5, 1.5)
    w_qkv = noise(splits[4], (D, 3 * HEADS * HD), D ** -0.5, 0.15625, ((0, 32),))
    w_pair = noise(splits[5], (D, 2 * CP), D ** -0.5, 0.15625, ((0, 32),))
    w_bias = draw_w_bias(jax.random.fold_in(splits[8], 71), 0)
    w_out = noise(splits[7], (HEADS * HD, D), (HEADS * HD) ** -0.5, 0.21875, ((1, 32),))
    return dict(bins=bins, pair_in=pair_in, valid=valid, gain=gain, w_qkv=w_qkv, w_pair=w_pair, w_bias=w_bias, w_out=w_out)


def one_window(bins, pair_in, valid, gain, w_qkv, w_pair, w_bias, w_out):
    feats = bins.astype(jnp.float32)
    meansq = lax.optimization_barrier(jnp.mean(feats * feats, axis=-1, keepdims=True))
    normed = (feats * lax.rsqrt(meansq + 1e-06) * gain).astype(jnp.bfloat16)
    proj = jnp.dot(normed, w_pair, preferred_element_type=jnp.float32)
    pooled = proj.reshape(PAIRS, POOL, 2 * CP).mean(axis=1).astype(jnp.bfloat16)
    left = pooled[:, :CP].astype(jnp.float32)
    right = pooled[:, CP:].astype(jnp.float32)
    pair_out = (pair_in.astype(jnp.float32) + left[:, None, :] * right[None, :, :]).astype(jnp.bfloat16)
    pbias = jnp.einsum('ijc,ch->hij', pair_out.astype(jnp.float32), w_bias)
    qkv = jnp.dot(normed, w_qkv, preferred_element_type=jnp.float32).astype(jnp.bfloat16)
    qkv = qkv.reshape(BINS, 3, HEADS, HD).astype(jnp.float32)
    query, keys, values = (qkv[:, 0], qkv[:, 1], qkv[:, 2])
    bias_full = jnp.repeat(jnp.repeat(pbias, POOL, axis=1), POOL, axis=2)
    scores = jnp.einsum('ihd,jhd->hij', query, keys) / jnp.sqrt(jnp.float32(HD)) + bias_full
    live = (jnp.arange(BINS) < valid)[None, None, :]
    scores = jnp.where(live, scores, jnp.float32(-1e+30))
    top = lax.optimization_barrier(jnp.max(scores, axis=-1, keepdims=True))
    expo = jnp.where(live, jnp.exp(scores - top), 0.0)
    total = lax.optimization_barrier(jnp.sum(expo, axis=-1))
    weights = expo.astype(jnp.bfloat16).astype(jnp.float32)
    attn = jnp.einsum('hij,jhd->hid', weights, values) / total[..., None]
    attn = jnp.transpose(attn, (1, 0, 2)).reshape(BINS, HEADS * HD).astype(jnp.bfloat16)
    mixed = (feats + jnp.dot(attn, w_out, preferred_element_type=jnp.float32)).astype(jnp.bfloat16)
    return (mixed, pair_out)

def reference(bins, pair_in, valid, gain, w_qkv, w_pair, w_bias, w_out):

    def step(items):
        return one_window(items[0], items[1], items[2], gain, w_qkv, w_pair, w_bias, w_out)
    mixed, pair_out = lax.map(step, (bins, pair_in, valid))
    return (mixed, pair_out)
```

```python
import functools

import jax
import jax.numpy as jnp
from jax import lax
from jax.experimental import pallas as pl
from jax.experimental.pallas import tpu as pltpu
from jax.sharding import Mesh, PartitionSpec as P

HEADS = 6
HD = 128
CP = 128
POOL = 16
HALF = HEADS // 2
HW = HALF * HD
VMEM = 48 * 1024 * 1024

BF = jnp.bfloat16
F32 = jnp.float32


def params():
    return pltpu.CompilerParams(vmem_limit_bytes=VMEM)


def vm():
    return pl.BlockSpec(memory_space=pltpu.VMEM)


def sm():
    return pl.BlockSpec(memory_space=pltpu.SMEM)


def hbm():
    return pl.BlockSpec(memory_space=pl.ANY)


def nt(a, b):
    return lax.dot_general(a, b, (((1,), (1,)), ((), ())), preferred_element_type=F32)


def weight_copies(place, own, other, buf, sem):
    nx, ny, rows = own.shape[0], own.shape[1], own.shape[2]
    me = place[1]
    copies = []
    for which, src in ((0, own), (1, other)):
        core = me if which == 0 else 1 - me
        for y in range(ny):
            for x in range(nx):
                at = ((y * nx + x) * 2 + core) * rows
                copies.append(
                    pltpu.make_async_copy(
                        src.at[x, y],
                        buf.at[pl.ds(pl.multiple_of(at, 16), rows), :],
                        sem.at[which, y * nx + x],
                    )
                )
    return copies


def norm_rows(x, gain):
    f = x.astype(F32)
    meansq = jnp.mean(f * f, axis=-1, keepdims=True)
    return (f * lax.rsqrt(meansq + 1e-06) * gain).astype(BF)


def kv_body(place, x_own, x_oth, gain, w_own, w_oth, kv, normed, buf, sem):
    copies = weight_copies(place, w_own, w_oth, buf, sem)
    for c in copies:
        c.start()
    rows = x_own.shape[0]
    side = place[0]
    g = gain[...]
    normed[pl.ds(pl.multiple_of(side * rows, 16), rows), :] = norm_rows(x_own[...], g)
    normed[pl.ds(pl.multiple_of((1 - side) * rows, 16), rows), :] = norm_rows(x_oth[...], g)
    for c in copies:
        c.wait()
    n = normed[...]
    kv[...] = jnp.dot(n, buf[...], preferred_element_type=F32).astype(BF)


def q_body(place, normed, w_own, w_oth, q, pooled, buf, sem):
    copies = weight_copies(place, w_own, w_oth, buf, sem)
    for c in copies:
        c.start()
    rows = normed.shape[0] // 2
    for c in copies:
        c.wait()
    own = normed[pl.ds(pl.multiple_of(place[0] * rows, 16), rows), :]
    second = jnp.dot(own, buf[:, : 2 * CP], preferred_element_type=F32)
    pooled[...] = second.reshape(rows // POOL, POOL, 2 * CP).mean(axis=1).astype(BF)
    q[...] = jnp.dot(normed[...], buf[:, 2 * CP :], preferred_element_type=F32).astype(BF)


def pair_body(pair_in, left, right, wt, pair_out, bias):
    r = right[...].astype(F32)
    w = wt[...]
    for i in range(pair_in.shape[0]):
        l = left[i : i + 1, :].astype(F32)
        out = (pair_in[i].astype(F32) + l * r).astype(BF)
        pair_out[i] = out
        both = nt(w, out)
        bias[i] = both[:8] + both[8:]


def split(x):
    hi = x.astype(BF)
    return hi, (x - hi.astype(F32)).astype(BF)


def attn_body(place, q, kvg, pb_own, pb_oth, mine, theirs):
    side = place[0]
    limit = place[2]
    nz, nrow = kvg.shape[0], kvg.shape[1]
    width = nz * nrow
    rows = nrow // 2
    half_bins = nz * rows
    npair = half_bins * 2 // POOL
    col = lax.broadcasted_iota(jnp.int32, (1, width), 1)
    z = col // nrow
    within = col % nrow
    bin_at = (within // rows) * half_bins + z * rows + within % rows
    live = bin_at < limit
    pair_at = bin_at // POOL
    onehot = (lax.broadcasted_iota(jnp.int32, (npair, width), 0) == pair_at).astype(F32).astype(BF)
    scale = 1.0 / (HD**0.5)
    own = pb_own[...]
    oth = pb_oth[...]
    for s in range(2):
        pb = jnp.where(side == s, own, oth)
        for h in range(HALF):
            qh = q[s * rows : (s + 1) * rows, h * HD : (h + 1) * HD]
            k = kvg[:, :, h * HD : (h + 1) * HD].reshape(width, HD)
            v = kvg[:, :, HW + h * HD : HW + (h + 1) * HD].reshape(width, HD)
            hi, lo = split(pb[:, h, :])
            bexp = jnp.dot(hi, onehot, preferred_element_type=F32) + jnp.dot(
                lo, onehot, preferred_element_type=F32
            )
            bexp = jnp.where(live, bexp, F32(-1e30))
            sc = nt(qh, k) * scale
            sc = (sc.reshape(rows // POOL, POOL, width) + bexp[:, None, :]).reshape(rows, width)
            top = jnp.max(sc, axis=-1, keepdims=True)
            e = jnp.exp(sc - top)
            total = jnp.sum(e, axis=-1, keepdims=True)
            acc = jnp.dot(e.astype(BF), v, preferred_element_type=F32)
            res = (acc / total).astype(BF)

            @pl.when(side == s)
            def _():
                mine[:, h * HD : (h + 1) * HD] = res

            @pl.when(side != s)
            def _():
                theirs[:, h * HD : (h + 1) * HD] = res


def out_body(place, x_own, a_own, a_oth, w_own, w_oth, mixed, buf, sem, full):
    copies = weight_copies(place, w_own, w_oth, buf, sem)
    for c in copies:
        c.start()
    side = place[0]
    full[:, pl.ds(pl.multiple_of(side * HW, 128), HW)] = a_own[...]
    full[:, pl.ds(pl.multiple_of((1 - side) * HW, 128), HW)] = a_oth[...]
    for c in copies:
        c.wait()
    update = nt(full[...], buf[...])
    mixed[...] = (x_own[...].astype(F32) + update).astype(BF)


def spread(x, axis, n):
    return lax.all_to_all(jnp.broadcast_to(x[None], (n,) + x.shape), axis, 0, 0, tiled=True)


def on_device(sizes, bins, pair_in, valid, gain, w_qkv, w_pair, w_bias, w_out):
    ny, nx, nz = sizes
    side = lax.axis_index("yh")
    core = lax.axis_index("c")
    swap = [(0, 1), (1, 0)]
    place = jnp.stack([side, core, valid[0]]).astype(jnp.int32)
    x_own = bins[0]
    rows, depth = x_own.shape
    shard = w_qkv.shape[0]
    x_oth = lax.ppermute(x_own, "yh", swap)

    def gather(w):
        w = spread(spread(w, "yl", ny), "x", nx)
        return w, lax.ppermute(w, "c", swap)

    def mine(first):
        return lax.dynamic_slice_in_dim(w_qkv, first * HEADS * HD + side * HW, HW, axis=1)

    kv_own, kv_oth = gather(jnp.concatenate([mine(1), mine(2)], axis=1))
    buf_sem = lambda n: [pltpu.VMEM((depth, n), BF), pltpu.SemaphoreType.DMA((2, nx * ny))]
    kv, normed = pl.pallas_call(
        kv_body,
        out_shape=(
            jax.ShapeDtypeStruct((2 * rows, 2 * HW), BF),
            jax.ShapeDtypeStruct((2 * rows, depth), BF),
        ),
        in_specs=[sm(), vm(), vm(), vm(), hbm(), hbm()],
        out_specs=(vm(), vm()),
        scratch_shapes=buf_sem(2 * HW),
        compiler_params=params(),
        name="kv",
    )(place, x_own, x_oth, gain[None], kv_own, kv_oth)
    kvg = lax.all_gather(kv, "z", axis=0)

    pq_own, pq_oth = gather(jnp.concatenate([w_pair, mine(0)], axis=1))
    q, pooled = pl.pallas_call(
        q_body,
        out_shape=(
            jax.ShapeDtypeStruct((2 * rows, HW), BF),
            jax.ShapeDtypeStruct((rows // POOL, 2 * CP), BF),
        ),
        in_specs=[sm(), vm(), hbm(), hbm()],
        out_specs=(vm(), vm()),
        scratch_shapes=buf_sem(2 * CP + HW),
        compiler_params=params(),
        name="q",
    )(place, normed, pq_own, pq_oth)
    right = spread(pooled[:, CP:], ("yh", "z"), 2 * nz).reshape(-1, CP)
    wt = w_bias.T
    zero = jnp.zeros((1, CP), F32)
    own_heads = lax.dynamic_slice_in_dim(wt, side * HALF, HALF, axis=0)
    oth_heads = lax.dynamic_slice_in_dim(wt, (1 - side) * HALF, HALF, axis=0)
    wt = jnp.concatenate([own_heads, zero, oth_heads, zero], axis=0)
    wt = jnp.concatenate(split(wt), axis=0)
    npr = pair_in.shape[1]
    pair_out, bias = pl.pallas_call(
        pair_body,
        out_shape=(
            jax.ShapeDtypeStruct(pair_in.shape[1:], BF),
            jax.ShapeDtypeStruct((npr, 8, pair_in.shape[2]), F32),
        ),
        in_specs=[vm()] * 4,
        out_specs=(vm(), vm()),
        compiler_params=params(),
        name="pair",
    )(pair_in[0], pooled[:, :CP], right, wt)
    pb_oth = lax.ppermute(bias[:, 4:], "yh", swap)

    wo_own, wo_oth = gather(w_out.T)
    mine_rows, their_rows = pl.pallas_call(
        attn_body,
        out_shape=(jax.ShapeDtypeStruct((rows, HW), BF),) * 2,
        in_specs=[sm(), vm(), vm(), vm(), vm()],
        out_specs=(vm(), vm()),
        compiler_params=params(),
        name="attn",
    )(place, q, kvg, bias[:, :4], pb_oth)
    got = lax.ppermute(their_rows, "yh", swap)
    mixed = pl.pallas_call(
        out_body,
        out_shape=jax.ShapeDtypeStruct((rows, depth), BF),
        in_specs=[sm(), vm(), vm(), vm(), hbm(), hbm()],
        out_specs=vm(),
        scratch_shapes=buf_sem(HEADS * HD) + [pltpu.VMEM((rows, HEADS * HD), BF)],
        compiler_params=params(),
        name="out",
    )(place, x_own, mine_rows, got, wo_own, wo_oth)
    return (mixed[None], pair_out[None])


def solution(mesh):
    fine = Mesh(mesh.devices.reshape(4, 4, 2, 2, 8), ("yl", "x", "c", "yh", "z"))
    dp, seq = ("yl", "x", "c"), ("yh", "z")
    placed = (
        P(dp, seq, None),
        P(dp, seq, None, None),
        P(dp),
        P(),
        P(dp, None),
        P(dp, None),
        P(),
        P(None, dp),
    )
    return jax.shard_map(
        functools.partial(on_device, (4, 4, 8)),
        mesh=fine,
        in_specs=placed,
        out_specs=(P(dp, seq, None), P(dp, seq, None, None)),
        check_vma=False,
    )
```

```python
import functools

import jax
import jax.numpy as jnp
from jax import lax
from jax.experimental import pallas as pl
from jax.experimental.pallas import tpu as pltpu
from jax.sharding import Mesh, PartitionSpec as P

HEADS = 6
HD = 128
CP = 128
POOL = 16
HALF = HEADS // 2
HW = HALF * HD
VMEM = 48 * 1024 * 1024

BF = jnp.bfloat16
F32 = jnp.float32

AXES = ("yl", "xh", "xl", "c", "yh", "zh", "zl")
SIZES = (4, 2, 2, 2, 2, 4, 2)
DP, X, SEQ = AXES[:4], AXES[1:3], AXES[4:]
NY, NX = 4, 4


def params():
    return pltpu.CompilerParams(vmem_limit_bytes=VMEM)


def vm():
    return pl.BlockSpec(memory_space=pltpu.VMEM)


def sm():
    return pl.BlockSpec(memory_space=pltpu.SMEM)


def hbm():
    return pl.BlockSpec(memory_space=pl.ANY)


def nt(a, b):
    return lax.dot_general(a, b, (((1,), (1,)), ((), ())), preferred_element_type=F32)


def split(x):
    hi = x.astype(BF)
    return hi, (x - hi.astype(F32)).astype(BF)


def weight_copies(place, own, other, buf, sem, across):
    rows = own.shape[2]
    me = place[1]
    copies = []
    for which, src in ((0, own), (1, other)):
        core = me if which == 0 else 1 - me
        for y in range(NY):
            for x in range(NX):
                at = ((y * NX + x) * 2 + core) * rows
                copies.append(
                    pltpu.make_async_copy(
                        src.at[x, y] if across else src.at[y, x],
                        buf.at[pl.ds(pl.multiple_of(at, 16), rows), :],
                        sem.at[which, y * NX + x],
                    )
                )
    return copies


def norm_rows(x, gain):
    f = x.astype(F32)
    meansq = jnp.mean(f * f, axis=-1, keepdims=True)
    return (f * lax.rsqrt(meansq + 1e-06) * gain).astype(BF)


def norm_body(place, x_own, near, far, gain, normed, means):
    rows, depth = x_own.shape
    side = place[0]
    g = gain[...]
    n = norm_rows(x_own[...], g).astype(F32)
    hi, lo = split(n.reshape(rows // POOL, POOL, depth).mean(axis=1))
    means[...] = jnp.concatenate([hi, lo], axis=0)
    normed[pl.ds(pl.multiple_of(side * rows, 16), rows), :] = norm_rows(near[...], g)
    normed[pl.ds(pl.multiple_of((1 - side) * rows, 16), rows), :] = norm_rows(far[...], g)


def kv_body(place, normed, means, w_own, w_oth, kv, pooled, buf, sem):
    copies = weight_copies(place, w_own, w_oth, buf, sem, True)
    for c in copies:
        c.start()
    for c in copies:
        c.wait()
    kv[...] = jnp.dot(normed[...], buf[:, : 2 * HW], preferred_element_type=F32).astype(BF)
    both = jnp.dot(means[...], buf[:, 2 * HW :], preferred_element_type=F32)
    n = both.shape[0] // 2
    pooled[...] = (both[:n] + both[n:]).astype(BF)


def q_body(place, normed, w_own, w_oth, q, buf, sem):
    copies = weight_copies(place, w_own, w_oth, buf, sem, False)
    for c in copies:
        c.start()
    for c in copies:
        c.wait()
    q[...] = jnp.dot(normed[...], buf[...], preferred_element_type=F32).astype(BF)


def pair_body(place, pair_in, left, right, wt, pair_out, bias):
    r = right[...].astype(F32)
    w = wt[...]
    limit = place[2].astype(F32)
    row = lax.broadcasted_iota(jnp.int32, (8, r.shape[0]), 0)
    spare = (row == 3) | (row == 7)
    for i in range(pair_in.shape[0]):
        l = left[i : i + 1, :].astype(F32)
        out = (pair_in[i].astype(F32) + l * r).astype(BF)
        pair_out[i] = out
        both = nt(w, out)
        bias[i] = jnp.where(spare, limit, both[:8] + both[8:])


def attn_body(place, q, kv_own, kv_oth, pb_near, pb_far, near, far):
    side = place[0]
    core = place[1]
    nchip, nrow = kv_own.shape[0], kv_own.shape[1]
    width = nchip * nrow
    rows = nrow // 2
    half_bins = 2 * nchip * rows
    npair = half_bins * 2 // POOL
    limit = pb_near[0:1, 3, 0:1]
    scale = 1.0 / (HD**0.5)

    col = lax.broadcasted_iota(jnp.int32, (1, width), 1)
    chip = col // nrow
    within = col % nrow
    pairs = lax.broadcasted_iota(jnp.int32, (npair, width), 0)
    live, onehot = [], []
    for cc in (core, 1 - core):
        z = (chip // 2) * 4 + cc * 2 + chip % 2
        bin_at = (within // rows) * half_bins + z * rows + within % rows
        live.append(bin_at.astype(F32) < limit)
        onehot.append((pairs == bin_at // POOL).astype(F32).astype(BF))
    pbn = pb_near[...]
    pbf = pb_far[...]
    for s in range(2):
        pb = jnp.where(side == s, pbn, pbf)
        for h in range(HALF):
            qh = q[s * rows : (s + 1) * rows, h * HD : (h + 1) * HD]
            hi, lo = split(pb[:, h, :])
            scores = []
            for kv, ok, hot in ((kv_own, live[0], onehot[0]), (kv_oth, live[1], onehot[1])):
                k = kv[:, :, h * HD : (h + 1) * HD].reshape(width, HD)
                bexp = jnp.dot(hi, hot, preferred_element_type=F32) + jnp.dot(
                    lo, hot, preferred_element_type=F32
                )
                bexp = jnp.where(ok, bexp, F32(-1e30))
                sc = nt(qh, k) * scale
                sc = sc.reshape(rows // POOL, POOL, width) + bexp[:, None, :]
                scores.append(sc.reshape(rows, width))
            top = jnp.maximum(
                jnp.max(scores[0], axis=-1, keepdims=True),
                jnp.max(scores[1], axis=-1, keepdims=True),
            )
            total, acc = 0.0, 0.0
            for sc, kv in zip(scores, (kv_own, kv_oth)):
                v = kv[:, :, HW + h * HD : HW + (h + 1) * HD].reshape(width, HD)
                e = jnp.exp(sc - top)
                total += jnp.sum(e, axis=-1, keepdims=True)
                acc += jnp.dot(e.astype(BF), v, preferred_element_type=F32)
            res = (acc / total).astype(BF)

            @pl.when(side == s)
            def _():
                near[:, h * HD : (h + 1) * HD] = res

            @pl.when(side != s)
            def _():
                far[:, h * HD : (h + 1) * HD] = res


def out_body(place, x_own, a_near, a_far, w_own, w_oth, mixed, buf, sem, full):
    copies = weight_copies(place, w_own, w_oth, buf, sem, False)
    for c in copies:
        c.start()
    side = place[0]
    full[:, pl.ds(pl.multiple_of(side * HW, 128), HW)] = a_near[...]
    full[:, pl.ds(pl.multiple_of((1 - side) * HW, 128), HW)] = a_far[...]
    for c in copies:
        c.wait()
    update = nt(full[...], buf[...])
    mixed[...] = (x_own[...].astype(F32) + update).astype(BF)


def spread(x, axis, n):
    return lax.all_to_all(jnp.broadcast_to(x[None], (n,) + x.shape), axis, 0, 0, tiled=True)


def core_swap(x):
    return lax.ppermute(x, "c", [(0, 1), (1, 0)])


def relocate(x, flip):
    moves = []
    for xl in range(2):
        for c in range(2):
            for yh in range(2):
                for zh in range(4):
                    here = ((xl * 2 + c) * 2 + yh) * 4 + zh
                    there = ((zh // 2 * 2 + zh % 2) * 2 + (yh ^ flip)) * 4 + xl * 2 + c
                    moves.append((here, there))
    return lax.ppermute(x, ("xl", "c", "yh", "zh"), moves)


def after(x, *others):
    return lax.optimization_barrier((x,) + others)[0]


def on_device(bins, pair_in, valid, gain, w_qkv, w_pair, w_bias, w_out):
    side = lax.axis_index("yh")
    core = lax.axis_index("c")
    place = jnp.stack([side, core, valid[0]]).astype(jnp.int32)
    x_own = bins[0]
    rows, depth = x_own.shape

    def mine(first):
        return lax.dynamic_slice_in_dim(w_qkv, first * HEADS * HD + side * HW, HW, axis=1)

    def weights(n):
        return [pltpu.VMEM((depth, n), BF), pltpu.SemaphoreType.DMA((2, NX * NY))]

    x_near = relocate(x_own, 0)
    x_far = relocate(x_own, 1)
    w = jnp.concatenate([mine(1), mine(2), w_pair], axis=1)
    w = spread(spread(w, "yl", NY), X, NX)
    normed, means = pl.pallas_call(
        norm_body,
        out_shape=(
            jax.ShapeDtypeStruct((2 * rows, depth), BF),
            jax.ShapeDtypeStruct((2 * rows // POOL, depth), BF),
        ),
        in_specs=[sm(), vm(), vm(), vm(), vm()],
        out_specs=(vm(), vm()),
        compiler_params=params(),
        name="norm",
    )(place, x_own, x_near, x_far, gain[None])
    w = after(w, normed)
    w_oth = core_swap(w)
    q_own = spread(after(mine(0), w), ("yl",) + X, NY * NX).reshape(NY, NX, -1, HW)
    kv, pooled = pl.pallas_call(
        kv_body,
        out_shape=(
            jax.ShapeDtypeStruct((2 * rows, 2 * HW), BF),
            jax.ShapeDtypeStruct((rows // POOL, 2 * CP), BF),
        ),
        in_specs=[sm(), vm(), vm(), hbm(), hbm()],
        out_specs=(vm(), vm()),
        scratch_shapes=weights(2 * HW + 2 * CP),
        compiler_params=params(),
        name="kv",
    )(place, normed, means, w, w_oth)
    kv_own = spread(kv, ("xl", "zl"), 4)
    right = spread(pooled[:, CP:], SEQ, 16).reshape(-1, CP)

    q_own = after(q_own, kv)
    q_oth = core_swap(q_own)
    q = pl.pallas_call(
        q_body,
        out_shape=jax.ShapeDtypeStruct((2 * rows, HW), BF),
        in_specs=[sm(), vm(), hbm(), hbm()],
        out_specs=vm(),
        scratch_shapes=weights(HW),
        compiler_params=params(),
        name="q",
    )(place, normed, q_own, q_oth)

    wt = w_bias.T
    zero = jnp.zeros((1, CP), F32)
    own_heads = lax.dynamic_slice_in_dim(wt, side * HALF, HALF, axis=0)
    oth_heads = lax.dynamic_slice_in_dim(wt, (1 - side) * HALF, HALF, axis=0)
    wt = jnp.concatenate([own_heads, zero, oth_heads, zero], axis=0)
    wt = jnp.concatenate(split(wt), axis=0)
    npr = pair_in.shape[1]
    pair_out, bias = pl.pallas_call(
        pair_body,
        out_shape=(
            jax.ShapeDtypeStruct(pair_in.shape[1:], BF),
            jax.ShapeDtypeStruct((npr, 8, pair_in.shape[2]), F32),
        ),
        in_specs=[sm()] + [vm()] * 4,
        out_specs=(vm(), vm()),
        compiler_params=params(),
        name="pair",
    )(place, pair_in[0], pooled[:, :CP], right, wt)
    pb_near = relocate(bias[:, :4], 0)
    pb_far = relocate(bias[:, 4:], 1)

    wo = after(w_out.T, q_own)
    wo = spread(wo, ("yl",) + X, NY * NX).reshape(NY, NX, -1, HEADS * HD)
    kv_oth = core_swap(kv_own)
    near, far = pl.pallas_call(
        attn_body,
        out_shape=(jax.ShapeDtypeStruct((rows, HW), BF),) * 2,
        in_specs=[sm()] + [vm()] * 5,
        out_specs=(vm(), vm()),
        compiler_params=params(),
        name="attn",
    )(place, q, kv_own, kv_oth, pb_near, pb_far)
    a_near = relocate(near, 0)
    a_far = relocate(far, 1)
    wo_oth = core_swap(wo)
    mixed = pl.pallas_call(
        out_body,
        out_shape=jax.ShapeDtypeStruct((rows, depth), BF),
        in_specs=[sm(), vm(), vm(), vm(), hbm(), hbm()],
        out_specs=vm(),
        scratch_shapes=weights(HEADS * HD) + [pltpu.VMEM((rows, HEADS * HD), BF)],
        compiler_params=params(),
        name="out",
    )(place, x_own, a_near, a_far, wo, wo_oth)
    return (mixed[None], pair_out[None])


def solution(mesh):
    fine = Mesh(mesh.devices.reshape(SIZES), AXES)
    placed = (
        P(DP, SEQ, None),
        P(DP, SEQ, None, None),
        P(DP),
        P(),
        P(DP, None),
        P(DP, None),
        P(),
        P(None, DP),
    )
    return jax.shard_map(
        on_device,
        mesh=fine,
        in_specs=placed,
        out_specs=(P(DP, SEQ, None), P(DP, SEQ, None, None)),
        check_vma=False,
    )
```

```python
import functools

import jax
import jax.numpy as jnp
from jax import lax
from jax.experimental import pallas as pl
from jax.experimental.pallas import tpu as pltpu
from jax.sharding import Mesh, PartitionSpec as P

HEADS = 6
HD = 128
CP = 128
POOL = 16
HALF = HEADS // 2
HW = HALF * HD
VMEM = 48 * 1024 * 1024

BF = jnp.bfloat16
F32 = jnp.float32

AXES = ("yl", "x", "c", "yh", "z")
SIZES = (4, 4, 2, 2, 8)
DP, SEQ = AXES[:3], AXES[3:]
NY, NX = 4, 4


def params():
    return pltpu.CompilerParams(vmem_limit_bytes=VMEM)


def vm():
    return pl.BlockSpec(memory_space=pltpu.VMEM)


def sm():
    return pl.BlockSpec(memory_space=pltpu.SMEM)


def hbm():
    return pl.BlockSpec(memory_space=pl.ANY)


def nt(a, b):
    return lax.dot_general(a, b, (((1,), (1,)), ((), ())), preferred_element_type=F32)


def split(x):
    hi = x.astype(BF)
    return hi, (x - hi.astype(F32)).astype(BF)


def weight_copies(place, own, other, buf, sem, first):
    rows = own.shape[2]
    cols = pl.ds(first, buf.shape[1])
    copies = []
    for which, src in ((0, own), (1, other)):
        core = place[1] if which == 0 else 1 - place[1]
        for y in range(NY):
            for x in range(NX):
                at = ((y * NX + x) * 2 + core) * rows
                copies.append(
                    pltpu.make_async_copy(
                        src.at[x, y, :, cols],
                        buf.at[pl.ds(pl.multiple_of(at, 16), rows), :],
                        sem.at[which, y * NX + x],
                    )
                )
    return copies


def norm_rows(x, gain):
    f = x.astype(F32)
    meansq = jnp.mean(f * f, axis=-1, keepdims=True)
    return (f * lax.rsqrt(meansq + 1e-06) * gain).astype(BF)


def norm_body(x_own, x_oth, gain, normed, means):
    rows, depth = x_own.shape
    g = gain[...]
    parts = []
    for at, x in ((0, x_own), (rows, x_oth)):
        n = norm_rows(x[...], g)
        normed[at : at + rows, :] = n
        parts.append(n.astype(F32).reshape(rows // POOL, POOL, depth).mean(axis=1))
    hi, lo = split(jnp.concatenate(parts, axis=0))
    means[...] = jnp.concatenate([hi, lo], axis=0)


def kv_body(place, normed, means, w_own, w_oth, kv, left, buf, sem):
    copies = weight_copies(place, w_own, w_oth, buf, sem, 0)
    for c in copies:
        c.start()
    for c in copies:
        c.wait()
    n = normed.shape[0]
    kv[:n, :] = jnp.dot(normed[...], buf[:, : 2 * HW], preferred_element_type=F32).astype(BF)
    both = jnp.dot(means[...], buf[:, 2 * HW :], preferred_element_type=F32)
    m = both.shape[0] // 2
    pooled = (both[:m] + both[m:]).astype(BF)
    left[...] = pooled[:, :CP].astype(F32)
    kv[n:, :CP] = pooled[:, CP:]
    kv[n:, CP:] = jnp.zeros((m, 2 * HW - CP), BF)


def q_body(place, normed, w_own, w_oth, q, buf, sem):
    copies = weight_copies(place, w_own, w_oth, buf, sem, 0)
    for c in copies:
        c.start()
    for c in copies:
        c.wait()
    q[...] = jnp.dot(normed[...], buf[...], preferred_element_type=F32).astype(BF)


def attn_body(place, q, kvg, pair_own, pair_oth, left, wt, pair_out, own, oth):
    side = place[0]
    limit = place[2]
    nz = kvg.shape[0]
    rows = q.shape[0] // 2
    npr = rows // POOL
    nrow = 2 * rows
    width = nz * nrow
    half_bins = nz * rows
    npair = half_bins * 2 // POOL
    scale = 1.0 / (HD**0.5)

    slots = ([], [])
    for z in range(nz):
        r = kvg[z, nrow:, :CP].astype(F32)
        slots[0].append(r[:npr])
        slots[1].append(r[npr:])
    first, second = (jnp.concatenate(x, axis=0) for x in slots)
    right = jnp.concatenate(
        [jnp.where(side == 0, first, second), jnp.where(side == 0, second, first)], axis=0
    )
    w = wt[...]

    col = lax.broadcasted_iota(jnp.int32, (1, width), 1)
    within = col % nrow
    yh = jnp.where(within // rows == 0, side, 1 - side)
    bin_at = yh * half_bins + (col // nrow) * rows + within % rows
    live = bin_at < limit
    onehot = (lax.broadcasted_iota(jnp.int32, (npair, width), 0) == bin_at // POOL).astype(F32)
    onehot = onehot.astype(BF)

    for s, (pair, dest) in enumerate(((pair_own, own), (pair_oth, oth))):
        biases = []
        for i in range(npr):
            l = left[s * npr + i : s * npr + i + 1, :]
            out = (pair[i].astype(F32) + l * right).astype(BF)
            if s == 0:
                pair_out[i] = out
            both = nt(w, out)
            biases.append(both[:8] + both[8:])
        pb = jnp.stack(biases)
        for h in range(HALF):
            qh = q[s * rows : (s + 1) * rows, h * HD : (h + 1) * HD]
            k = kvg[:, :nrow, h * HD : (h + 1) * HD].reshape(width, HD)
            v = kvg[:, :nrow, HW + h * HD : HW + (h + 1) * HD].reshape(width, HD)
            hi, lo = split(pb[:, h, :])
            bexp = jnp.dot(hi, onehot, preferred_element_type=F32) + jnp.dot(
                lo, onehot, preferred_element_type=F32
            )
            bexp = jnp.where(live, bexp, F32(-1e30))
            sc = nt(qh, k) * scale
            sc = (sc.reshape(npr, POOL, width) + bexp[:, None, :]).reshape(rows, width)
            top = jnp.max(sc, axis=-1, keepdims=True)
            e = jnp.exp(sc - top)
            total = jnp.sum(e, axis=-1, keepdims=True)
            acc = jnp.dot(e.astype(BF), v, preferred_element_type=F32)
            dest[:, h * HD : (h + 1) * HD] = (acc / total).astype(BF)


def out_body(place, x_own, a_own, a_oth, w_own, w_oth, mixed, buf, sem, full):
    copies = weight_copies(place, w_own, w_oth, buf, sem, HW)
    for c in copies:
        c.start()
    side = place[0]
    full[:, pl.ds(pl.multiple_of(side * HW, 128), HW)] = a_own[...]
    full[:, pl.ds(pl.multiple_of((1 - side) * HW, 128), HW)] = a_oth[...]
    for c in copies:
        c.wait()
    update = nt(full[...], buf[...])
    mixed[...] = (x_own[...].astype(F32) + update).astype(BF)


def spread(x, axis, n):
    return lax.all_to_all(jnp.broadcast_to(x[None], (n,) + x.shape), axis, 0, 0, tiled=True)


def swap(x, axis):
    return lax.ppermute(x, axis, [(0, 1), (1, 0)])


def after(x, *others):
    return lax.optimization_barrier((x,) + others)[0]


def on_device(bins, pair_in, valid, gain, w_qkv, w_pair, w_bias, w_out):
    side = lax.axis_index("yh")
    core = lax.axis_index("c")
    place = jnp.stack([side, core, valid[0]]).astype(jnp.int32)
    x_own = bins[0]
    rows, depth = x_own.shape
    npr = rows // POOL

    def mine(first):
        return lax.dynamic_slice_in_dim(w_qkv, first * HEADS * HD + side * HW, HW, axis=1)

    def weights(n):
        return [pltpu.VMEM((depth, n), BF), pltpu.SemaphoreType.DMA((2, NX * NY))]

    x_oth = swap(x_own, "yh")
    pair_oth = swap(pair_in[0], "yh")
    w = jnp.concatenate([mine(1), mine(2), w_pair], axis=1)
    w = spread(spread(w, "yl", NY), "x", NX)
    normed, means = pl.pallas_call(
        norm_body,
        out_shape=(
            jax.ShapeDtypeStruct((2 * rows, depth), BF),
            jax.ShapeDtypeStruct((4 * npr, depth), BF),
        ),
        in_specs=[vm()] * 3,
        out_specs=(vm(), vm()),
        compiler_params=params(),
        name="norm",
    )(x_own, x_oth, gain[None])
    w = after(w, normed)
    w_oth = swap(w, "c")
    kv, left = pl.pallas_call(
        kv_body,
        out_shape=(
            jax.ShapeDtypeStruct((2 * rows + 2 * npr, 2 * HW), BF),
            jax.ShapeDtypeStruct((2 * npr, CP), F32),
        ),
        in_specs=[sm(), vm(), vm(), hbm(), hbm()],
        out_specs=(vm(), vm()),
        scratch_shapes=weights(2 * HW + 2 * CP),
        compiler_params=params(),
        name="kv",
    )(place, normed, means, w, w_oth)
    kvg = lax.all_gather(kv, "z", axis=0)

    u = jnp.concatenate([mine(0), w_out.T], axis=1)
    u = spread(spread(after(u, w), "yl", NY), "x", NX)
    u_oth = swap(u, "c")
    q = pl.pallas_call(
        q_body,
        out_shape=jax.ShapeDtypeStruct((2 * rows, HW), BF),
        in_specs=[sm(), vm(), hbm(), hbm()],
        out_specs=vm(),
        scratch_shapes=weights(HW),
        compiler_params=params(),
        name="q",
    )(place, normed, u, u_oth)

    wt = lax.dynamic_slice_in_dim(w_bias.T, side * HALF, HALF, axis=0)
    wt = jnp.concatenate([wt, jnp.zeros((8 - HALF, CP), F32)], axis=0)
    wt = jnp.concatenate(split(wt), axis=0)
    pair_out, own, oth = pl.pallas_call(
        attn_body,
        out_shape=(jax.ShapeDtypeStruct(pair_in.shape[1:], BF),)
        + (jax.ShapeDtypeStruct((rows, HW), BF),) * 2,
        in_specs=[sm()] + [vm()] * 6,
        out_specs=(vm(), vm(), vm()),
        compiler_params=params(),
        name="attn",
    )(place, q, kvg, pair_in[0], pair_oth, left, wt)
    got = swap(oth, "yh")
    mixed = pl.pallas_call(
        out_body,
        out_shape=jax.ShapeDtypeStruct((rows, depth), BF),
        in_specs=[sm(), vm(), vm(), vm(), hbm(), hbm()],
        out_specs=vm(),
        scratch_shapes=weights(HEADS * HD) + [pltpu.VMEM((rows, HEADS * HD), BF)],
        compiler_params=params(),
        name="out",
    )(place, x_own, own, got, u, u_oth)
    return (mixed[None], pair_out[None])


def solution(mesh):
    fine = Mesh(mesh.devices.reshape(SIZES), AXES)
    placed = (
        P(DP, SEQ, None),
        P(DP, SEQ, None, None),
        P(DP),
        P(),
        P(DP, None),
        P(DP, None),
        P(),
        P(None, DP),
    )
    return jax.shard_map(
        on_device,
        mesh=fine,
        in_specs=placed,
        out_specs=(P(DP, SEQ, None), P(DP, SEQ, None, None)),
        check_vma=False,
    )
```

```python
import functools

import jax
import jax.numpy as jnp
from jax import lax
from jax.experimental import pallas as pl
from jax.experimental.pallas import tpu as pltpu
from jax.sharding import Mesh, PartitionSpec as P

HEADS = 6
HD = 128
CP = 128
POOL = 16
HALF = HEADS // 2
HW = HALF * HD
VMEM = 14 * 1024 * 1024

BF = jnp.bfloat16
F32 = jnp.float32

AXES = ("yl", "x", "c", "yh", "z")
SIZES = (4, 4, 2, 2, 8)
DP, SEQ = AXES[:3], AXES[3:]
NY, NX = 4, 4


def params():
    return pltpu.CompilerParams(vmem_limit_bytes=VMEM)


def cost(gflop):
    return pl.CostEstimate(flops=gflop * 10**9, bytes_accessed=1 << 20, transcendentals=0)


def vm():
    return pl.BlockSpec(memory_space=pltpu.VMEM)


def sm():
    return pl.BlockSpec(memory_space=pltpu.SMEM)


def hbm():
    return pl.BlockSpec(memory_space=pl.ANY)


def nt(a, b):
    return lax.dot_general(a, b, (((1,), (1,)), ((), ())), preferred_element_type=F32)


def split(x):
    hi = x.astype(BF)
    return hi, (x - hi.astype(F32)).astype(BF)


def weight_copies(place, own, other, buf, sem, first):
    rows = own.shape[2]
    cols = pl.ds(first, buf.shape[1])
    copies = []
    for which, src in ((0, own), (1, other)):
        core = place[1] if which == 0 else 1 - place[1]
        for y in range(NY):
            for x in range(NX):
                at = ((y * NX + x) * 2 + core) * rows
                copies.append(
                    pltpu.make_async_copy(
                        src.at[x, y, :, cols],
                        buf.at[pl.ds(pl.multiple_of(at, 16), rows), :],
                        sem.at[which, y * NX + x],
                    )
                )
    return copies


def norm_rows(x, gain):
    f = x.astype(F32)
    meansq = jnp.mean(f * f, axis=-1, keepdims=True)
    return (f * lax.rsqrt(meansq + 1e-06) * gain).astype(BF)


def norm_body(x_own, x_oth, gain, normed, means):
    rows, depth = x_own.shape
    g = gain[...]
    parts = []
    for at, x in ((0, x_own), (rows, x_oth)):
        n = norm_rows(x[...], g)
        normed[at : at + rows, :] = n
        parts.append(n.astype(F32).reshape(rows // POOL, POOL, depth).mean(axis=1))
    hi, lo = split(jnp.concatenate(parts, axis=0))
    means[...] = jnp.concatenate([hi, lo], axis=0)


def kv_body(place, normed, means, w_own, w_oth, kv, left, buf, sem):
    copies = weight_copies(place, w_own, w_oth, buf, sem, 0)
    for c in copies:
        c.start()
    for c in copies:
        c.wait()
    n = normed.shape[0]
    kv[:n, :] = jnp.dot(normed[...], buf[:, : 2 * HW], preferred_element_type=F32).astype(BF)
    both = jnp.dot(means[...], buf[:, 2 * HW :], preferred_element_type=F32)
    m = both.shape[0] // 2
    pooled = (both[:m] + both[m:]).astype(BF)
    left[...] = pooled[:, :CP].astype(F32)
    kv[n:, :CP] = pooled[:, CP:]
    kv[n:, CP:] = jnp.zeros((m, 2 * HW - CP), BF)


def q_body(place, normed, w_own, w_oth, q, buf, sem):
    copies = weight_copies(place, w_own, w_oth, buf, sem, 0)
    for c in copies:
        c.start()
    for c in copies:
        c.wait()
    q[...] = jnp.dot(normed[...], buf[...], preferred_element_type=F32).astype(BF)


def attn_body(place, q_at, kvg_at, pair_own_at, pair_oth_at, left, wt, pair_out, own, oth, *held):
    refs, sem = held[:4], held[4]
    copies = [
        pltpu.make_async_copy(src, dst, sem.at[i])
        for i, (src, dst) in enumerate(zip((kvg_at, pair_own_at, pair_oth_at, q_at), refs))
    ]
    for c in copies:
        c.start()
    kvg, pair_own, pair_oth, q = refs
    side = place[0]
    limit = place[2]
    nz = kvg.shape[0]
    rows = q.shape[0] // 2
    npr = rows // POOL
    nrow = 2 * rows
    width = nz * nrow
    half_bins = nz * rows
    npair = half_bins * 2 // POOL
    scale = 1.0 / (HD**0.5)

    for c in copies:
        c.wait()
    slots = ([], [])
    for z in range(nz):
        r = kvg[z, nrow:, :CP].astype(F32)
        slots[0].append(r[:npr])
        slots[1].append(r[npr:])
    first, second = (jnp.concatenate(x, axis=0) for x in slots)
    right = jnp.concatenate(
        [jnp.where(side == 0, first, second), jnp.where(side == 0, second, first)], axis=0
    )
    w = wt[...]

    col = lax.broadcasted_iota(jnp.int32, (1, width), 1)
    within = col % nrow
    yh = jnp.where(within // rows == 0, side, 1 - side)
    bin_at = yh * half_bins + (col // nrow) * rows + within % rows
    live = bin_at < limit
    onehot = (lax.broadcasted_iota(jnp.int32, (npair, width), 0) == bin_at // POOL).astype(F32)
    onehot = onehot.astype(BF)

    for s, (pair, dest) in enumerate(((pair_own, own), (pair_oth, oth))):
        biases = []
        for i in range(npr):
            l = left[s * npr + i : s * npr + i + 1, :]
            out = (pair[i].astype(F32) + l * right).astype(BF)
            if s == 0:
                pair_out[i] = out
            both = nt(w, out)
            biases.append(both[:8] + both[8:])
        pb = jnp.stack(biases)
        for h in range(HALF):
            qh = q[s * rows : (s + 1) * rows, h * HD : (h + 1) * HD]
            k = kvg[:, :nrow, h * HD : (h + 1) * HD].reshape(width, HD)
            v = kvg[:, :nrow, HW + h * HD : HW + (h + 1) * HD].reshape(width, HD)
            hi, lo = split(pb[:, h, :])
            bexp = jnp.dot(hi, onehot, preferred_element_type=F32) + jnp.dot(
                lo, onehot, preferred_element_type=F32
            )
            bexp = jnp.where(live, bexp, F32(-1e30))
            sc = nt(qh, k) * scale
            sc = (sc.reshape(npr, POOL, width) + bexp[:, None, :]).reshape(rows, width)
            top = jnp.max(sc, axis=-1, keepdims=True)
            e = jnp.exp(sc - top)
            total = jnp.sum(e, axis=-1, keepdims=True)
            acc = jnp.dot(e.astype(BF), v, preferred_element_type=F32)
            dest[:, h * HD : (h + 1) * HD] = (acc / total).astype(BF)


def out_body(place, x_own, a_own, a_oth, w_own, w_oth, mixed, buf, sem, full):
    copies = weight_copies(place, w_own, w_oth, buf, sem, HW)
    for c in copies:
        c.start()
    side = place[0]
    full[:, pl.ds(pl.multiple_of(side * HW, 128), HW)] = a_own[...]
    full[:, pl.ds(pl.multiple_of((1 - side) * HW, 128), HW)] = a_oth[...]
    for c in copies:
        c.wait()
    update = nt(full[...], buf[...])
    mixed[...] = (x_own[...].astype(F32) + update).astype(BF)


def spread(x, axis, n):
    return lax.all_to_all(jnp.broadcast_to(x[None], (n,) + x.shape), axis, 0, 0, tiled=True)


def swap(x, axis):
    return lax.ppermute(x, axis, [(0, 1), (1, 0)])


def after(x, *others):
    return lax.optimization_barrier((x,) + others)[0]


def on_device(bins, pair_in, valid, gain, w_qkv, w_pair, w_bias, w_out):
    side = lax.axis_index("yh")
    core = lax.axis_index("c")
    place = jnp.stack([side, core, valid[0]]).astype(jnp.int32)
    x_own = bins[0]
    rows, depth = x_own.shape
    npr = rows // POOL

    def mine(first):
        return lax.dynamic_slice_in_dim(w_qkv, first * HEADS * HD + side * HW, HW, axis=1)

    def weights(n):
        return [pltpu.VMEM((depth, n), BF), pltpu.SemaphoreType.DMA((2, NX * NY))]

    x_oth = swap(x_own, "yh")
    w = jnp.concatenate([mine(1), mine(2), w_pair], axis=1)
    w = spread(spread(w, "yl", NY), "x", NX)
    normed, means = pl.pallas_call(
        norm_body,
        out_shape=(
            jax.ShapeDtypeStruct((2 * rows, depth), BF),
            jax.ShapeDtypeStruct((4 * npr, depth), BF),
        ),
        in_specs=[vm()] * 3,
        out_specs=(vm(), vm()),
        compiler_params=params(),
        cost_estimate=cost(20),
        name="norm",
    )(x_own, x_oth, gain[None])
    w_oth = swap(w, "c")
    kv, left = pl.pallas_call(
        kv_body,
        out_shape=(
            jax.ShapeDtypeStruct((2 * rows + 2 * npr, 2 * HW), BF),
            jax.ShapeDtypeStruct((2 * npr, CP), F32),
        ),
        in_specs=[sm(), vm(), vm(), hbm(), hbm()],
        out_specs=(vm(), vm()),
        scratch_shapes=weights(2 * HW + 2 * CP),
        compiler_params=params(),
        cost_estimate=cost(10),
        name="kv",
    )(place, normed, means, w, w_oth)
    kvg = lax.all_gather(kv, "z", axis=0)

    u = jnp.concatenate([mine(0), w_out.T], axis=1)
    u = spread(after(u, w), "yl", NY)
    pair_oth = swap(after(pair_in[0], u), "yh")
    u = spread(u, "x", NX)
    u_oth = swap(after(u, pair_oth), "c")
    q = pl.pallas_call(
        q_body,
        out_shape=jax.ShapeDtypeStruct((2 * rows, HW), BF),
        in_specs=[sm(), vm(), hbm(), hbm()],
        out_specs=vm(),
        scratch_shapes=weights(HW),
        compiler_params=params(),
        name="q",
    )(place, normed, u, u_oth)

    wt = lax.dynamic_slice_in_dim(w_bias.T, side * HALF, HALF, axis=0)
    wt = jnp.concatenate([wt, jnp.zeros((8 - HALF, CP), F32)], axis=0)
    wt = jnp.concatenate(split(wt), axis=0)
    pair_out, own, oth = pl.pallas_call(
        attn_body,
        out_shape=(jax.ShapeDtypeStruct(pair_in.shape[1:], BF),)
        + (jax.ShapeDtypeStruct((rows, HW), BF),) * 2,
        in_specs=[sm()] + [hbm()] * 4 + [vm()] * 2,
        out_specs=(vm(), vm(), vm()),
        scratch_shapes=[pltpu.VMEM(x.shape, BF) for x in (kvg, pair_oth, pair_oth, q)]
        + [pltpu.SemaphoreType.DMA((4,))],
        compiler_params=pltpu.CompilerParams(vmem_limit_bytes=56 * 1024 * 1024),
        cost_estimate=cost(10),
        name="attn",
    )(place, q, kvg, pair_in[0], pair_oth, left, wt)
    got = swap(oth, "yh")
    mixed = pl.pallas_call(
        out_body,
        out_shape=jax.ShapeDtypeStruct((rows, depth), BF),
        in_specs=[sm(), vm(), vm(), vm(), hbm(), hbm()],
        out_specs=vm(),
        scratch_shapes=weights(HEADS * HD) + [pltpu.VMEM((rows, HEADS * HD), BF)],
        compiler_params=params(),
        name="out",
    )(place, x_own, own, got, u, u_oth)
    return (mixed[None], pair_out[None])


def solution(mesh):
    fine = Mesh(mesh.devices.reshape(SIZES), AXES)
    placed = (
        P(DP, SEQ, None),
        P(DP, SEQ, None, None),
        P(DP),
        P(),
        P(DP, None),
        P(DP, None),
        P(),
        P(None, DP),
    )
    return jax.shard_map(
        on_device,
        mesh=fine,
        in_specs=placed,
        out_specs=(P(DP, SEQ, None), P(DP, SEQ, None, None)),
        check_vma=False,
    )
```

```python
import functools

import jax
import jax.numpy as jnp
from jax import lax
from jax.experimental import pallas as pl
from jax.experimental.pallas import tpu as pltpu
from jax.sharding import Mesh, PartitionSpec as P

HEADS = 6
HD = 128
CP = 128
POOL = 16
HALF = HEADS // 2
HW = HALF * HD
VMEM = 14 * 1024 * 1024

BF = jnp.bfloat16
F32 = jnp.float32

AXES = ("yl", "x", "c", "yh", "z")
SIZES = (4, 4, 2, 2, 8)
DP, SEQ = AXES[:3], AXES[3:]
NY, NX, NZ = 4, 4, 8


def params():
    return pltpu.CompilerParams(vmem_limit_bytes=VMEM)


def cost(gflop):
    return pl.CostEstimate(flops=gflop * 10**9, bytes_accessed=1 << 20, transcendentals=0)


def vm():
    return pl.BlockSpec(memory_space=pltpu.VMEM)


def sm():
    return pl.BlockSpec(memory_space=pltpu.SMEM)


def hbm():
    return pl.BlockSpec(memory_space=pl.ANY)


def nt(a, b):
    return lax.dot_general(a, b, (((1,), (1,)), ((), ())), preferred_element_type=F32)


def split(x):
    hi = x.astype(BF)
    return hi, (x - hi.astype(F32)).astype(BF)


def weight_copies(place, own, other, buf, sem):
    return [
        pltpu.make_async_copy(src.at[x], buf.at[:, x, core], sem.at[which, x])
        for which, src, core in ((0, own, place[1]), (1, other, 1 - place[1]))
        for x in range(NX)
    ]


def rows_of(buf):
    x = buf[...]
    return x.reshape(-1, x.shape[-1])


def project(means, w):
    both = jnp.dot(means, w, preferred_element_type=F32)
    half = both.shape[0] // 2
    return (both[:half] + both[half:]).astype(BF)


def norm_rows(x, gain):
    f = x.astype(F32)
    meansq = jnp.mean(f * f, axis=-1, keepdims=True)
    return (f * lax.rsqrt(meansq + 1e-06) * gain).astype(BF)


def norm_body(x_own, x_oth, gain, normed, means):
    rows, depth = x_own.shape
    g = gain[...]
    parts = []
    for at, x in ((0, x_own), (rows, x_oth)):
        n = norm_rows(x[...], g)
        normed[at : at + rows, :] = n
        parts.append(n.astype(F32).reshape(rows // POOL, POOL, depth).mean(axis=1))
    hi, lo = split(jnp.concatenate(parts, axis=0))
    means[...] = jnp.concatenate([hi, lo], axis=0)


def kv_body(place, normed, means, w_own, w_oth, kv, buf, sem):
    copies = weight_copies(place, w_own, w_oth, buf, sem)
    for c in copies:
        c.start()
    for c in copies:
        c.wait()
    w = rows_of(buf)
    n = normed.shape[0]
    kv[:n, :] = jnp.dot(normed[...], w[:, : 2 * HW], preferred_element_type=F32).astype(BF)
    right = project(means[...], w[:, 2 * HW :])
    kv[n:, :CP] = right
    kv[n:, CP:] = jnp.zeros((right.shape[0], 2 * HW - CP), BF)


def q_body(place, normed, means, w_own, w_oth, q, left, buf, sem):
    copies = weight_copies(place, w_own, w_oth, buf, sem)
    for c in copies:
        c.start()
    for c in copies:
        c.wait()
    w = rows_of(buf)
    q[...] = jnp.dot(normed[...], w[:, CP:], preferred_element_type=F32).astype(BF)
    left[...] = project(means[...], w[:, :CP]).astype(F32)


def pair_bias_body(pair_in, wt, bias):
    w = wt[...]
    for i in range(pair_in.shape[0]):
        both = nt(w, pair_in[i])
        bias[i] = both[:8] + both[8:]


def attn_body(place, q_at, kvg_at, pair_own_at, bias_oth, left, wt, wt32, pair_out, own, oth, *held):
    feats, pair_own, q, kvg, sem = held
    rows = q.shape[0] // 2
    copies = [
        pltpu.make_async_copy(src, dst, sem.at[i])
        for i, (src, dst) in enumerate(
            (
                (kvg_at.at[:, pl.ds(2 * rows, feats.shape[1]), pl.ds(0, CP)], feats),
                (pair_own_at, pair_own),
                (q_at, q),
                (kvg_at.at[:, pl.ds(0, 2 * rows), :], kvg),
            )
        )
    ]
    for c in copies:
        c.start()
    side = place[0]
    limit = place[2]
    nz = kvg.shape[0]
    npr = rows // POOL
    nrow = 2 * rows
    width = nz * nrow
    half_bins = nz * rows
    npair = half_bins * 2 // POOL
    scale = 1.0 / (HD**0.5)

    for c in copies[:2]:
        c.wait()
    slots = ([], [])
    for z in range(nz):
        r = feats[z].astype(F32)
        slots[0].append(r[:npr])
        slots[1].append(r[npr:])
    first, second = (jnp.concatenate(x, axis=0) for x in slots)
    right = jnp.concatenate(
        [jnp.where(side == 0, first, second), jnp.where(side == 0, second, first)], axis=0
    )
    w = wt[...]

    col = lax.broadcasted_iota(jnp.int32, (1, width), 1)
    within = col % nrow
    yh = jnp.where(within // rows == 0, side, 1 - side)
    bin_at = yh * half_bins + (col // nrow) * rows + within % rows
    live = bin_at < limit
    onehot = (lax.broadcasted_iota(jnp.int32, (npair, width), 0) == bin_at // POOL).astype(F32)
    onehot = onehot.astype(BF)

    biases = []
    for i in range(npr):
        out = (pair_own[i].astype(F32) + left[i : i + 1, :] * right).astype(BF)
        pair_out[i] = out
        both = nt(w, out)
        biases.append(both[:8] + both[8:])
    biases = [jnp.stack(biases)]
    lw = (left[npr:, :][:, None, :] * wt32[...][None, :, :]).reshape(8 * npr, CP)
    feats_bf = right.astype(BF)
    hi, lo = split(lw)
    biases.append(bias_oth[...] + (nt(hi, feats_bf) + nt(lo, feats_bf)).reshape(npr, 8, npair))
    parts = [pb[:, h, :] for pb in biases for h in range(HALF)]
    hi, lo = split(jnp.concatenate(parts, axis=0))
    bias = jnp.dot(hi, onehot, preferred_element_type=F32) + jnp.dot(lo, onehot, preferred_element_type=F32)
    bias = jnp.where(live, bias, F32(-1e30))
    for c in copies[2:]:
        c.wait()

    for h in range(HALF):
        k = kvg[:, :, h * HD : (h + 1) * HD].reshape(width, HD)
        v = kvg[:, :, HW + h * HD : HW + (h + 1) * HD].reshape(width, HD)
        for s, dest in enumerate((own, oth)):
            qh = q[s * rows : (s + 1) * rows, h * HD : (h + 1) * HD]
            first = (s * HALF + h) * npr
            sc = nt(qh, k) * scale
            sc = sc.reshape(npr, POOL, width) + bias[first : first + npr, None, :]
            sc = sc.reshape(rows, width)
            top = jnp.max(sc, axis=-1, keepdims=True)
            e = jnp.exp(sc - top)
            total = jnp.sum(e, axis=-1, keepdims=True)
            acc = jnp.dot(e.astype(BF), v, preferred_element_type=F32)
            dest[:, h * HD : (h + 1) * HD] = (acc / total).astype(BF)


def out_body(place, x_own, a_own, a_oth, w_own, w_oth, mixed, buf, sem, full):
    copies = weight_copies(place, w_own, w_oth, buf, sem)
    for c in copies:
        c.start()
    side = place[0]
    full[:, pl.ds(pl.multiple_of(side * HW, 128), HW)] = a_own[...]
    full[:, pl.ds(pl.multiple_of((1 - side) * HW, 128), HW)] = a_oth[...]
    for c in copies:
        c.wait()
    update = nt(full[...], rows_of(buf))
    mixed[...] = (x_own[...].astype(F32) + update).astype(BF)


def spread(x, axis, n):
    return lax.all_to_all(jnp.broadcast_to(x[None], (n,) + x.shape), axis, 0, 0, tiled=True)


def swap(x, axis):
    return lax.ppermute(x, axis, [(0, 1), (1, 0)])


def after(x, *others):
    return lax.optimization_barrier((x,) + others)[0]


def on_device(bins, pair_in, valid, gain, w_qkv, w_pair, w_bias, w_out):
    side = lax.axis_index("yh")
    core = lax.axis_index("c")
    place = jnp.stack([side, core, valid[0]]).astype(jnp.int32)
    x_own = bins[0]
    rows, depth = x_own.shape
    npr = rows // POOL
    shard = w_qkv.shape[0]

    def mine(first):
        return lax.dynamic_slice_in_dim(w_qkv, first * HEADS * HD + side * HW, HW, axis=1)

    def weights(n):
        return [pltpu.VMEM((NY, NX, 2, shard, n), BF), pltpu.SemaphoreType.DMA((2, NX))]

    def heads(at):
        x = lax.dynamic_slice_in_dim(w_bias.T, at * HALF, HALF, axis=0)
        x = jnp.concatenate([x, jnp.zeros((8 - HALF, CP), F32)], axis=0)
        return x, jnp.concatenate(split(x), axis=0)

    wt32, wt = heads(side)
    bias_for_oth = pl.pallas_call(
        pair_bias_body,
        out_shape=jax.ShapeDtypeStruct((npr, 8, pair_in.shape[2]), F32),
        in_specs=[vm()] * 2,
        out_specs=vm(),
        compiler_params=params(),
        name="pair_bias",
    )(pair_in[0], heads(1 - side)[1])

    x_oth = swap(x_own, "yh")
    w = jnp.concatenate([mine(1), mine(2), w_pair[:, CP:]], axis=1)
    w = spread(spread(w, "yl", NY), "x", NX)
    normed, means = pl.pallas_call(
        norm_body,
        out_shape=(
            jax.ShapeDtypeStruct((2 * rows, depth), BF),
            jax.ShapeDtypeStruct((4 * npr, depth), BF),
        ),
        in_specs=[vm()] * 3,
        out_specs=(vm(), vm()),
        compiler_params=params(),
        cost_estimate=cost(20),
        name="norm",
    )(x_own, x_oth, gain[None])
    w_oth = swap(w, "c")
    kv = pl.pallas_call(
        kv_body,
        out_shape=jax.ShapeDtypeStruct((2 * rows + 2 * npr, 2 * HW), BF),
        in_specs=[sm(), vm(), vm(), hbm(), hbm()],
        out_specs=vm(),
        scratch_shapes=weights(2 * HW + CP),
        compiler_params=params(),
        cost_estimate=cost(10),
        name="kv",
    )(place, normed, means, w, w_oth)
    kvg = lax.all_gather(kv, "z", axis=0)

    u = jnp.concatenate([w_pair[:, :CP], mine(0), w_out.T], axis=1)
    u = spread(after(u, w), "yl", NY)
    bias_oth = swap(after(bias_for_oth, u), "yh")
    u, wo = u[:, :, : CP + HW], u[:, :, CP + HW :]
    u = after(spread(u, "x", NX), bias_oth)
    q, left = pl.pallas_call(
        q_body,
        out_shape=(jax.ShapeDtypeStruct((2 * rows, HW), BF), jax.ShapeDtypeStruct((2 * npr, CP), F32)),
        in_specs=[sm(), vm(), vm(), hbm(), hbm()],
        out_specs=(vm(), vm()),
        scratch_shapes=weights(CP + HW),
        compiler_params=params(),
        name="q",
    )(place, normed, means, u, swap(u, "c"))
    wo = spread(after(wo, u), "x", NX)

    pair_out, own, oth = pl.pallas_call(
        attn_body,
        out_shape=(jax.ShapeDtypeStruct(pair_in.shape[1:], BF),)
        + (jax.ShapeDtypeStruct((rows, HW), BF),) * 2,
        in_specs=[sm()] + [hbm()] * 3 + [vm()] * 4,
        out_specs=(vm(), vm(), vm()),
        scratch_shapes=[
            pltpu.VMEM(shape, BF)
            for shape in (
                (NZ, 2 * npr, CP),
                pair_in.shape[1:],
                q.shape,
                (NZ, 2 * rows, 2 * HW),
            )
        ]
        + [pltpu.SemaphoreType.DMA((4,))],
        compiler_params=pltpu.CompilerParams(vmem_limit_bytes=56 * 1024 * 1024),
        cost_estimate=cost(10),
        name="attn",
    )(place, q, kvg, pair_in[0], bias_oth, left, wt, wt32)
    got = swap(oth, "yh")
    wo_oth = swap(after(wo, oth), "c")
    mixed = pl.pallas_call(
        out_body,
        out_shape=jax.ShapeDtypeStruct((rows, depth), BF),
        in_specs=[sm(), vm(), vm(), vm(), hbm(), hbm()],
        out_specs=vm(),
        scratch_shapes=weights(HEADS * HD) + [pltpu.VMEM((rows, HEADS * HD), BF)],
        compiler_params=params(),
        name="out",
    )(place, x_own, own, got, wo, wo_oth)
    return (mixed[None], pair_out[None])


def solution(mesh):
    fine = Mesh(mesh.devices.reshape(SIZES), AXES)
    placed = (
        P(DP, SEQ, None),
        P(DP, SEQ, None, None),
        P(DP),
        P(),
        P(DP, None),
        P(DP, None),
        P(),
        P(None, DP),
    )
    return jax.shard_map(
        on_device,
        mesh=fine,
        in_specs=placed,
        out_specs=(P(DP, SEQ, None), P(DP, SEQ, None, None)),
        check_vma=False,
    )
```

```python
import functools

import jax
import jax.numpy as jnp
from jax import lax
from jax.experimental import pallas as pl
from jax.experimental.pallas import tpu as pltpu
from jax.sharding import Mesh, PartitionSpec as P

HEADS = 6
HD = 128
CP = 128
POOL = 16
HALF = HEADS // 2
HW = HALF * HD
VMEM = 14 * 1024 * 1024

BF = jnp.bfloat16
F32 = jnp.float32

AXES = ("yl", "x", "c", "yh", "z")
SIZES = (4, 4, 2, 2, 8)
DP, SEQ = AXES[:3], AXES[3:]
NY, NX, NZ = 4, 4, 8


def params():
    return pltpu.CompilerParams(vmem_limit_bytes=VMEM)


def cost(gflop):
    return pl.CostEstimate(flops=gflop * 10**9, bytes_accessed=1 << 20, transcendentals=0)


def vm():
    return pl.BlockSpec(memory_space=pltpu.VMEM)


def sm():
    return pl.BlockSpec(memory_space=pltpu.SMEM)


def hbm():
    return pl.BlockSpec(memory_space=pl.ANY)


def nt(a, b):
    return lax.dot_general(a, b, (((1,), (1,)), ((), ())), preferred_element_type=F32)


def split(x):
    hi = x.astype(BF)
    return hi, (x - hi.astype(F32)).astype(BF)


def weight_copies(place, own, other, buf, sem):
    return [
        pltpu.make_async_copy(src.at[x], buf.at[:, x, core], sem.at[which, x])
        for which, src, core in ((0, own, place[1]), (1, other, 1 - place[1]))
        for x in range(NX)
    ]


def rows_of(buf):
    x = buf[...]
    return x.reshape(-1, x.shape[-1])


def project(means, w):
    both = jnp.dot(means, w, preferred_element_type=F32)
    half = both.shape[0] // 2
    return (both[:half] + both[half:]).astype(BF)


def norm_rows(x, gain):
    f = x.astype(F32)
    meansq = jnp.mean(f * f, axis=-1, keepdims=True)
    return (f * lax.rsqrt(meansq + 1e-06) * gain).astype(BF)


def norm_body(x_own, x_oth, gain, normed, means):
    rows, depth = x_own.shape
    g = gain[...]
    parts = []
    for at, x in ((0, x_own), (rows, x_oth)):
        n = norm_rows(x[...], g)
        normed[at : at + rows, :] = n
        parts.append(n.astype(F32).reshape(rows // POOL, POOL, depth).mean(axis=1))
    hi, lo = split(jnp.concatenate(parts, axis=0))
    means[...] = jnp.concatenate([hi, lo], axis=0)


def kv_body(place, normed, means, w_own, w_oth, kv, buf, sem):
    copies = weight_copies(place, w_own, w_oth, buf, sem)
    for c in copies:
        c.start()
    for c in copies:
        c.wait()
    w = rows_of(buf)
    n = normed.shape[0]
    both = jnp.dot(normed[...], w[:, : 2 * HW], preferred_element_type=F32).astype(BF)
    for i in range(2 * HALF):
        kv[i * n : (i + 1) * n, :] = both[:, i * HD : (i + 1) * HD]
    kv[2 * HALF * n :, :] = project(means[...], w[:, 2 * HW :])


def q_body(place, normed, means, w_own, w_oth, q, left, buf, sem):
    copies = weight_copies(place, w_own, w_oth, buf, sem)
    for c in copies:
        c.start()
    for c in copies:
        c.wait()
    w = rows_of(buf)
    q[...] = jnp.dot(normed[...], w[:, CP:], preferred_element_type=F32).astype(BF)
    left[...] = project(means[...], w[:, :CP]).astype(F32)


def head_weights(w, at):
    x = jnp.where(at == 0, w[:HALF, :], w[HALF:, :])
    x = jnp.concatenate([x, jnp.zeros((8 - HALF, x.shape[1]), F32)], axis=0)
    return x, jnp.concatenate(split(x), axis=0)


def pair_bias_body(place, pair_in, w_bias, bias):
    w = head_weights(w_bias[...], 1 - place[0])[1]
    for i in range(pair_in.shape[0]):
        both = nt(w, pair_in[i])
        bias[i] = both[:8] + both[8:]


def attn_body(place, *refs):
    q_at, kvg_at, pair_at, bias_at, left_at, w_at, pair_out_at, own, oth = refs[:9]
    feats, pair_own, q, kvg, bias_oth, left, w_bias, pair_out, sem, sem_out = refs[9:]
    rows = q.shape[0] // 2
    copies = [
        pltpu.make_async_copy(src, dst, sem.at[i])
        for i, (src, dst) in enumerate(
            (
                (kvg_at.at[:, pl.ds(4 * HALF * rows, feats.shape[1]), :], feats),
                (pair_at, pair_own),
                (bias_at, bias_oth),
                (left_at, left),
                (w_at, w_bias),
                (q_at, q),
            )
            + tuple(
                (kvg_at.at[:, pl.ds(2 * rows * i, 2 * rows), :], kvg.at[i])
                for h in range(HALF)
                for i in (h, HALF + h)
            )
        )
    ]
    for c in copies:
        c.start()
    side = place[0]
    limit = place[2]
    nz = kvg.shape[1]
    npr = rows // POOL
    nrow = 2 * rows
    width = nz * nrow
    half_bins = nz * rows
    npair = half_bins * 2 // POOL
    scale = 1.0 / (HD**0.5)
    log2e = 1.4426950408889634

    for c in copies[:5]:
        c.wait()
    slots = ([], [])
    for z in range(nz):
        r = feats[z].astype(F32)
        slots[0].append(r[:npr])
        slots[1].append(r[npr:])
    first, second = (jnp.concatenate(x, axis=0) for x in slots)
    right = jnp.concatenate(
        [jnp.where(side == 0, first, second), jnp.where(side == 0, second, first)], axis=0
    )
    w32, w = head_weights(w_bias[...], side)

    col = lax.broadcasted_iota(jnp.int32, (1, width), 1)
    within = col % nrow
    yh = jnp.where(within // rows == 0, side, 1 - side)
    bin_at = yh * half_bins + (col // nrow) * rows + within % rows
    live = bin_at < limit
    onehot = (lax.broadcasted_iota(jnp.int32, (npair, width), 0) == bin_at // POOL).astype(F32)
    onehot = onehot.astype(BF)

    outs = []
    for i in range(npr):
        out = (pair_own[i].astype(F32) + left[i : i + 1, :] * right).astype(BF)
        pair_out[i] = out
        outs.append(out)
    written = pltpu.make_async_copy(pair_out, pair_out_at, sem_out.at[0])
    written.start()
    both = nt(w, jnp.concatenate(outs, axis=0))
    both = both[:8] + both[8:]
    biases = [jnp.stack([both[:, i * npair : (i + 1) * npair] for i in range(npr)])]
    lw = (left[npr:, :][:, None, :] * w32[None, :, :]).reshape(8 * npr, CP)
    feats_bf = right.astype(BF)
    hi, lo = split(lw)
    biases.append(bias_oth[...] + (nt(hi, feats_bf) + nt(lo, feats_bf)).reshape(npr, 8, npair))
    parts = [pb[:, h, :] for h in range(HALF) for pb in biases]
    hi, lo = split(jnp.concatenate(parts, axis=0) * (1.0 / scale))
    bias = jnp.dot(jnp.concatenate([hi, lo], axis=0), onehot, preferred_element_type=F32)
    bias = bias[: hi.shape[0]] + bias[hi.shape[0] :]
    bias = jnp.where(live, bias, F32(-1e30))
    copies[5].wait()

    for h in range(HALF):
        cols = slice(h * HD, (h + 1) * HD)
        for c in copies[6 + 2 * h : 8 + 2 * h]:
            c.wait()
        k = kvg[h].reshape(width, HD)
        v = kvg[HALF + h].reshape(width, HD)
        sc = nt(q[:, cols], k).reshape(2 * npr, POOL, width)
        sc = (sc + bias[2 * h * npr : 2 * (h + 1) * npr, None, :]).reshape(2 * rows, width)
        top = jnp.max(sc, axis=-1, keepdims=True)
        e = jnp.exp2((sc - top) * (scale * log2e))
        total = jnp.sum(e, axis=-1, keepdims=True)
        acc = jnp.dot(e.astype(BF), v, preferred_element_type=F32)
        res = (acc / total).astype(BF)
        own[:, cols] = res[:rows]
        oth[:, cols] = res[rows:]
    written.wait()


def out_body(place, x_at, a_own, a_oth, w_own, w_oth, mixed, buf, sem, full, x_own, sem_x):
    copies = weight_copies(place, w_own, w_oth, buf, sem)
    copies.append(pltpu.make_async_copy(x_at, x_own, sem_x.at[0]))
    for c in copies:
        c.start()
    side = place[0]
    full[:, pl.ds(pl.multiple_of(side * HW, 128), HW)] = a_own[...]
    full[:, pl.ds(pl.multiple_of((1 - side) * HW, 128), HW)] = a_oth[...]
    for c in copies:
        c.wait()
    update = nt(full[...], rows_of(buf))
    mixed[...] = (x_own[...].astype(F32) + update).astype(BF)


def spread(x, axis, n):
    return lax.all_to_all(jnp.broadcast_to(x[None], (n,) + x.shape), axis, 0, 0, tiled=True)


def swap(x, axis):
    return lax.ppermute(x, axis, [(0, 1), (1, 0)])


def after(x, *others):
    return lax.optimization_barrier((x,) + others)[0]


def on_device(bins, pair_in, valid, gain, w_qkv, w_pair, w_bias, w_out):
    side = lax.axis_index("yh")
    core = lax.axis_index("c")
    place = jnp.stack([side, core, valid[0]]).astype(jnp.int32)
    x_own = bins[0]
    rows, depth = x_own.shape
    npr = rows // POOL
    shard = w_qkv.shape[0]

    def mine(first):
        return lax.dynamic_slice_in_dim(w_qkv, first * HEADS * HD + side * HW, HW, axis=1)

    def weights(n):
        return [pltpu.VMEM((NY, NX, 2, shard, n), BF), pltpu.SemaphoreType.DMA((2, NX))]

    bias_for_oth = pl.pallas_call(
        pair_bias_body,
        out_shape=jax.ShapeDtypeStruct((npr, 8, pair_in.shape[2]), F32),
        in_specs=[sm(), vm(), vm()],
        out_specs=vm(),
        compiler_params=params(),
        name="pair_bias",
    )(place, pair_in[0], w_bias.T)

    x_oth = swap(x_own, "yh")
    w = jnp.concatenate([mine(1), mine(2), w_pair[:, CP:]], axis=1)
    w = spread(spread(w, "yl", NY), "x", NX)
    normed, means = pl.pallas_call(
        norm_body,
        out_shape=(
            jax.ShapeDtypeStruct((2 * rows, depth), BF),
            jax.ShapeDtypeStruct((4 * npr, depth), BF),
        ),
        in_specs=[vm()] * 3,
        out_specs=(vm(), vm()),
        compiler_params=params(),
        cost_estimate=cost(20),
        name="norm",
    )(x_own, x_oth, gain[None])
    w_oth = swap(w, "c")
    kv = pl.pallas_call(
        kv_body,
        out_shape=jax.ShapeDtypeStruct((4 * HALF * rows + 2 * npr, HD), BF),
        in_specs=[sm(), vm(), vm(), hbm(), hbm()],
        out_specs=vm(),
        scratch_shapes=weights(2 * HW + CP),
        compiler_params=params(),
        cost_estimate=cost(10),
        name="kv",
    )(place, normed, means, w, w_oth)
    kvg = lax.all_gather(kv, "z", axis=0)

    u = jnp.concatenate([w_pair[:, :CP], mine(0), w_out.T], axis=1)
    u = spread(after(u, w), "yl", NY)
    bias_oth = swap(after(bias_for_oth, u), "yh")
    u, wo = u[:, :, : CP + HW], u[:, :, CP + HW :]
    u = after(spread(u, "x", NX), bias_oth)
    q, left = pl.pallas_call(
        q_body,
        out_shape=(jax.ShapeDtypeStruct((2 * rows, HW), BF), jax.ShapeDtypeStruct((2 * npr, CP), F32)),
        in_specs=[sm(), vm(), vm(), hbm(), hbm()],
        out_specs=(vm(), vm()),
        scratch_shapes=weights(CP + HW),
        compiler_params=params(),
        name="q",
    )(place, normed, means, u, swap(u, "c"))
    wo = spread(after(wo, u), "x", NX)

    pair_out, own, oth = pl.pallas_call(
        attn_body,
        out_shape=(jax.ShapeDtypeStruct(pair_in.shape[1:], BF),)
        + (jax.ShapeDtypeStruct((rows, HW), BF),) * 2,
        in_specs=[sm()] + [hbm()] * 6,
        out_specs=(hbm(), vm(), vm()),
        scratch_shapes=[
            pltpu.VMEM((NZ, 2 * npr, CP), BF),
            pltpu.VMEM(pair_in.shape[1:], BF),
            pltpu.VMEM(q.shape, BF),
            pltpu.VMEM((2 * HALF, NZ, 2 * rows, HD), BF),
            pltpu.VMEM(bias_oth.shape, F32),
            pltpu.VMEM(left.shape, F32),
            pltpu.VMEM((HEADS, CP), F32),
            pltpu.VMEM(pair_in.shape[1:], BF),
            pltpu.SemaphoreType.DMA((6 + 2 * HALF,)),
            pltpu.SemaphoreType.DMA((1,)),
        ],
        compiler_params=pltpu.CompilerParams(vmem_limit_bytes=56 * 1024 * 1024),
        cost_estimate=cost(10),
        name="attn",
    )(place, q, kvg, pair_in[0], bias_oth, left, w_bias.T)
    got = swap(oth, "yh")
    wo_oth = swap(after(wo, oth), "c")
    mixed = pl.pallas_call(
        out_body,
        out_shape=jax.ShapeDtypeStruct((rows, depth), BF),
        in_specs=[sm(), hbm(), vm(), vm(), hbm(), hbm()],
        out_specs=vm(),
        scratch_shapes=weights(HEADS * HD)
        + [
            pltpu.VMEM((rows, HEADS * HD), BF),
            pltpu.VMEM((rows, depth), BF),
            pltpu.SemaphoreType.DMA((1,)),
        ],
        compiler_params=params(),
        name="out",
    )(place, x_own, own, got, wo, wo_oth)
    return (mixed[None], pair_out[None])


def solution(mesh):
    fine = Mesh(mesh.devices.reshape(SIZES), AXES)
    placed = (
        P(DP, SEQ, None),
        P(DP, SEQ, None, None),
        P(DP),
        P(),
        P(DP, None),
        P(DP, None),
        P(),
        P(None, DP),
    )
    return jax.shard_map(
        on_device,
        mesh=fine,
        in_specs=placed,
        out_specs=(P(DP, SEQ, None), P(DP, SEQ, None, None)),
        check_vma=False,
    )
```

```python
import functools

import jax
import jax.numpy as jnp
from jax import lax
from jax.experimental import pallas as pl
from jax.experimental.pallas import tpu as pltpu
from jax.sharding import Mesh, PartitionSpec as P

HEADS = 6
HD = 128
CP = 128
POOL = 16
HALF = HEADS // 2
HW = HALF * HD
VMEM = 14 * 1024 * 1024

BF = jnp.bfloat16
F32 = jnp.float32

AXES = ("yl", "x", "c", "yh", "z")
SIZES = (4, 4, 2, 2, 8)
DP, SEQ = AXES[:3], AXES[3:]
NY, NX, NZ = 4, 4, 8


def params():
    return pltpu.CompilerParams(vmem_limit_bytes=VMEM)


def cost(gflop):
    return pl.CostEstimate(flops=gflop * 10**9, bytes_accessed=1 << 20, transcendentals=0)


def vm():
    return pl.BlockSpec(memory_space=pltpu.VMEM)


def sm():
    return pl.BlockSpec(memory_space=pltpu.SMEM)


def hbm():
    return pl.BlockSpec(memory_space=pl.ANY)


def nt(a, b):
    return lax.dot_general(a, b, (((1,), (1,)), ((), ())), preferred_element_type=F32)


def split(x):
    hi = x.astype(BF)
    return hi, (x - hi.astype(F32)).astype(BF)


def weight_copies(place, own, other, buf, sem):
    return [
        pltpu.make_async_copy(src.at[x], buf.at[:, x, core], sem.at[which, x])
        for which, src, core in ((0, own, place[1]), (1, other, 1 - place[1]))
        for x in range(NX)
    ]


def rows_of(buf):
    x = buf[...]
    return x.reshape(-1, x.shape[-1])


def project(means, w):
    both = jnp.dot(means, w, preferred_element_type=F32)
    half = both.shape[0] // 2
    return (both[:half] + both[half:]).astype(BF)


def norm_rows(x, gain):
    f = x.astype(F32)
    meansq = jnp.mean(f * f, axis=-1, keepdims=True)
    return (f * lax.rsqrt(meansq + 1e-06) * gain).astype(BF)


def norm_body(x_own, x_oth, gain, normed, means):
    rows, depth = x_own.shape
    g = gain[...]
    parts = []
    for at, x in ((0, x_own), (rows, x_oth)):
        n = norm_rows(x[...], g)
        normed[at : at + rows, :] = n
        parts.append(n.astype(F32).reshape(rows // POOL, POOL, depth).mean(axis=1))
    hi, lo = split(jnp.concatenate(parts, axis=0))
    means[...] = jnp.concatenate([hi, lo], axis=0)


def kv_body(place, normed, means, w_own, w_oth, kv, buf, sem):
    copies = [
        pltpu.make_async_copy(src.at[:, y], buf.at[y, :, core], sem.at[which, y])
        for y in range(NY)
        for which, src, core in ((0, w_own, place[1]), (1, w_oth, 1 - place[1]))
    ]
    for c in copies:
        c.start()
    n = normed.shape[0]
    m = means.shape[0] // 2
    depth = normed.shape[1] // NY
    both, pooled = 0.0, 0.0
    for y in range(NY):
        for c in copies[2 * y : 2 * y + 2]:
            c.wait()
        w = buf[y].reshape(depth, buf.shape[-1])
        part = slice(y * depth, (y + 1) * depth)
        both += jnp.dot(normed[:, part], w[:, : 2 * HW], preferred_element_type=F32)
        pooled += jnp.dot(means[:, part], w[:, 2 * HW :], preferred_element_type=F32)
    both = both.astype(BF)
    for i in range(2 * HALF):
        kv[i * n : (i + 1) * n, :] = both[:, i * HD : (i + 1) * HD]
    kv[2 * HALF * n :, :] = (pooled[:m] + pooled[m:]).astype(BF)


def q_body(place, normed, means, w_own, w_oth, q, left, buf, sem):
    copies = weight_copies(place, w_own, w_oth, buf, sem)
    for c in copies:
        c.start()
    for c in copies:
        c.wait()
    w = rows_of(buf)
    q[...] = jnp.dot(normed[...], w[:, CP:], preferred_element_type=F32).astype(BF)
    left[...] = project(means[...], w[:, :CP]).astype(F32)


def head_weights(w, at):
    x = jnp.where(at == 0, w[:HALF, :], w[HALF:, :])
    x = jnp.concatenate([x, jnp.zeros((8 - HALF, x.shape[1]), F32)], axis=0)
    return x, jnp.concatenate(split(x), axis=0)


def pair_bias_body(place, pair_in, w_bias, bias):
    w = head_weights(w_bias[...], 1 - place[0])[1]
    for i in range(pair_in.shape[0]):
        both = nt(w, pair_in[i])
        bias[i] = both[:8] + both[8:]


def attn_body(place, *refs):
    q_at, kvg_at, pair_at, bias_at, left_at, w_at, pair_out_at, own, oth = refs[:9]
    feats, pair_own, q, kvg, bias_oth, left, w_bias, pair_out, sem, sem_out = refs[9:]
    rows = q.shape[0] // 2
    copies = [
        pltpu.make_async_copy(src, dst, sem.at[i])
        for i, (src, dst) in enumerate(
            (
                (kvg_at.at[:, pl.ds(4 * HALF * rows, feats.shape[1]), :], feats),
                (pair_at, pair_own),
                (bias_at, bias_oth),
                (left_at, left),
                (w_at, w_bias),
                (q_at, q),
            )
            + tuple(
                (kvg_at.at[:, pl.ds(2 * rows * i, 2 * rows), :], kvg.at[i])
                for h in range(HALF)
                for i in (h, HALF + h)
            )
        )
    ]
    for c in copies:
        c.start()
    side = place[0]
    limit = place[2]
    nz = kvg.shape[1]
    npr = rows // POOL
    nrow = 2 * rows
    width = nz * nrow
    half_bins = nz * rows
    npair = half_bins * 2 // POOL
    scale = 1.0 / (HD**0.5)
    log2e = 1.4426950408889634

    for c in copies[:5]:
        c.wait()
    slots = ([], [])
    for z in range(nz):
        r = feats[z].astype(F32)
        slots[0].append(r[:npr])
        slots[1].append(r[npr:])
    first, second = (jnp.concatenate(x, axis=0) for x in slots)
    right = jnp.concatenate(
        [jnp.where(side == 0, first, second), jnp.where(side == 0, second, first)], axis=0
    )
    w32, w = head_weights(w_bias[...], side)

    col = lax.broadcasted_iota(jnp.int32, (1, width), 1)
    within = col % nrow
    yh = jnp.where(within // rows == 0, side, 1 - side)
    bin_at = yh * half_bins + (col // nrow) * rows + within % rows
    live = bin_at < limit
    onehot = (lax.broadcasted_iota(jnp.int32, (npair, width), 0) == bin_at // POOL).astype(F32)
    onehot = onehot.astype(BF)

    outs = []
    for i in range(npr):
        out = (pair_own[i].astype(F32) + left[i : i + 1, :] * right).astype(BF)
        pair_out[i] = out
        outs.append(out)
    written = pltpu.make_async_copy(pair_out, pair_out_at, sem_out.at[0])
    written.start()
    both = nt(w, jnp.concatenate(outs, axis=0))
    both = both[:8] + both[8:]
    biases = [jnp.stack([both[:, i * npair : (i + 1) * npair] for i in range(npr)])]
    lw = (left[npr:, :][:, None, :] * w32[None, :, :]).reshape(8 * npr, CP)
    feats_bf = right.astype(BF)
    hi, lo = split(lw)
    biases.append(bias_oth[...] + (nt(hi, feats_bf) + nt(lo, feats_bf)).reshape(npr, 8, npair))
    parts = [pb[:, h, :] for h in range(HALF) for pb in biases]
    hi, lo = split(jnp.concatenate(parts, axis=0) * (1.0 / scale))
    bias = jnp.dot(jnp.concatenate([hi, lo], axis=0), onehot, preferred_element_type=F32)
    bias = bias[: hi.shape[0]] + bias[hi.shape[0] :]
    bias = jnp.where(live, bias, F32(-1e30))
    copies[5].wait()

    for h in range(HALF):
        cols = slice(h * HD, (h + 1) * HD)
        for c in copies[6 + 2 * h : 8 + 2 * h]:
            c.wait()
        k = kvg[h].reshape(width, HD)
        v = kvg[HALF + h].reshape(width, HD)
        sc = nt(q[:, cols], k).reshape(2 * npr, POOL, width)
        sc = (sc + bias[2 * h * npr : 2 * (h + 1) * npr, None, :]).reshape(2 * rows, width)
        top = jnp.max(sc, axis=-1, keepdims=True)
        e = jnp.exp2((sc - top) * (scale * log2e))
        total = jnp.sum(e, axis=-1, keepdims=True)
        acc = jnp.dot(e.astype(BF), v, preferred_element_type=F32)
        res = (acc / total).astype(BF)
        own[:, cols] = res[:rows]
        oth[:, cols] = res[rows:]
    written.wait()


def out_body(place, x_at, a_own, a_oth, w_own, w_oth, mixed, buf, sem, full, x_own, sem_x):
    copies = weight_copies(place, w_own, w_oth, buf, sem)
    copies.append(pltpu.make_async_copy(x_at, x_own, sem_x.at[0]))
    for c in copies:
        c.start()
    side = place[0]
    full[:, pl.ds(pl.multiple_of(side * HW, 128), HW)] = a_own[...]
    full[:, pl.ds(pl.multiple_of((1 - side) * HW, 128), HW)] = a_oth[...]
    for c in copies:
        c.wait()
    update = nt(full[...], rows_of(buf))
    mixed[...] = (x_own[...].astype(F32) + update).astype(BF)


def spread(x, axis, n):
    return lax.all_to_all(jnp.broadcast_to(x[None], (n,) + x.shape), axis, 0, 0, tiled=True)


def swap(x, axis):
    return lax.ppermute(x, axis, [(0, 1), (1, 0)])


def after(x, *others):
    return lax.optimization_barrier((x,) + others)[0]


def on_device(bins, pair_in, valid, gain, w_qkv, w_pair, w_bias, w_out):
    side = lax.axis_index("yh")
    core = lax.axis_index("c")
    place = jnp.stack([side, core, valid[0]]).astype(jnp.int32)
    x_own = bins[0]
    rows, depth = x_own.shape
    npr = rows // POOL
    shard = w_qkv.shape[0]

    def mine(first):
        return lax.dynamic_slice_in_dim(w_qkv, first * HEADS * HD + side * HW, HW, axis=1)

    def weights(n):
        return [pltpu.VMEM((NY, NX, 2, shard, n), BF), pltpu.SemaphoreType.DMA((2, NX))]

    bias_for_oth = pl.pallas_call(
        pair_bias_body,
        out_shape=jax.ShapeDtypeStruct((npr, 8, pair_in.shape[2]), F32),
        in_specs=[sm(), vm(), vm()],
        out_specs=vm(),
        compiler_params=params(),
        name="pair_bias",
    )(place, pair_in[0], w_bias.T)

    x_oth = swap(x_own, "yh")
    w = jnp.concatenate([mine(1), mine(2), w_pair[:, CP:]], axis=1)
    w = spread(spread(w, "yl", NY), "x", NX)
    normed, means = pl.pallas_call(
        norm_body,
        out_shape=(
            jax.ShapeDtypeStruct((2 * rows, depth), BF),
            jax.ShapeDtypeStruct((4 * npr, depth), BF),
        ),
        in_specs=[vm()] * 3,
        out_specs=(vm(), vm()),
        compiler_params=params(),
        cost_estimate=cost(20),
        name="norm",
    )(x_own, x_oth, gain[None])
    w_oth = swap(w, "c")
    kv = pl.pallas_call(
        kv_body,
        out_shape=jax.ShapeDtypeStruct((4 * HALF * rows + 2 * npr, HD), BF),
        in_specs=[sm(), vm(), vm(), hbm(), hbm()],
        out_specs=vm(),
        scratch_shapes=weights(2 * HW + CP),
        compiler_params=params(),
        cost_estimate=cost(10),
        name="kv",
    )(place, normed, means, w, w_oth)
    kvg = lax.all_gather(kv, "z", axis=0)

    u = jnp.concatenate([w_pair[:, :CP], mine(0), w_out.T], axis=1)
    u = spread(after(u, w), "yl", NY)
    bias_oth = swap(after(bias_for_oth, u), "yh")
    u, wo = u[:, :, : CP + HW], u[:, :, CP + HW :]
    u = after(spread(u, "x", NX), bias_oth)
    q, left = pl.pallas_call(
        q_body,
        out_shape=(jax.ShapeDtypeStruct((2 * rows, HW), BF), jax.ShapeDtypeStruct((2 * npr, CP), F32)),
        in_specs=[sm(), vm(), vm(), hbm(), hbm()],
        out_specs=(vm(), vm()),
        scratch_shapes=weights(CP + HW),
        compiler_params=params(),
        name="q",
    )(place, normed, means, u, swap(u, "c"))
    wo = spread(after(wo, u), "x", NX)

    pair_out, own, oth = pl.pallas_call(
        attn_body,
        out_shape=(jax.ShapeDtypeStruct(pair_in.shape[1:], BF),)
        + (jax.ShapeDtypeStruct((rows, HW), BF),) * 2,
        in_specs=[sm()] + [hbm()] * 6,
        out_specs=(hbm(), vm(), vm()),
        scratch_shapes=[
            pltpu.VMEM((NZ, 2 * npr, CP), BF),
            pltpu.VMEM(pair_in.shape[1:], BF),
            pltpu.VMEM(q.shape, BF),
            pltpu.VMEM((2 * HALF, NZ, 2 * rows, HD), BF),
            pltpu.VMEM(bias_oth.shape, F32),
            pltpu.VMEM(left.shape, F32),
            pltpu.VMEM((HEADS, CP), F32),
            pltpu.VMEM(pair_in.shape[1:], BF),
            pltpu.SemaphoreType.DMA((6 + 2 * HALF,)),
            pltpu.SemaphoreType.DMA((1,)),
        ],
        compiler_params=pltpu.CompilerParams(vmem_limit_bytes=56 * 1024 * 1024),
        cost_estimate=cost(10),
        name="attn",
    )(place, q, kvg, pair_in[0], bias_oth, left, w_bias.T)
    got = swap(oth, "yh")
    wo_oth = swap(after(wo, oth), "c")
    mixed = pl.pallas_call(
        out_body,
        out_shape=jax.ShapeDtypeStruct((rows, depth), BF),
        in_specs=[sm(), hbm(), vm(), vm(), hbm(), hbm()],
        out_specs=vm(),
        scratch_shapes=weights(HEADS * HD)
        + [
            pltpu.VMEM((rows, HEADS * HD), BF),
            pltpu.VMEM((rows, depth), BF),
            pltpu.SemaphoreType.DMA((1,)),
        ],
        compiler_params=params(),
        name="out",
    )(place, x_own, own, got, wo, wo_oth)
    return (mixed[None], pair_out[None])


def solution(mesh):
    fine = Mesh(mesh.devices.reshape(SIZES), AXES)
    placed = (
        P(DP, SEQ, None),
        P(DP, SEQ, None, None),
        P(DP),
        P(),
        P(DP, None),
        P(DP, None),
        P(),
        P(None, DP),
    )
    return jax.shard_map(
        on_device,
        mesh=fine,
        in_specs=placed,
        out_specs=(P(DP, SEQ, None), P(DP, SEQ, None, None)),
        check_vma=False,
    )
```
